32 devices in a mesh: clip: 2 (over x), trow: 8 (over z, y), tcol: 2 (over core).
Axes of the slice: x: 2, y: 2, z: 4, core: 2. Of those that a mesh axis runs over, the one named last changes fastest.
Arguments:
- field: bfloat16 [8, 2048, 8192], P(None, ('clip', 'trow'), 'tcol'), parts along dimension 1, may hold values from -6 to 6
- pointwise: bfloat16 [2, 8, 8], replicated, may hold values from -2 to 2
- mixing: bfloat16 [2, 2, 8, 8, 4608], replicated, may hold values from -2 to 2
- project: bfloat16 [8], replicated, may hold values from -2 to 2
Outputs:
- image: bfloat16 [2048, 8192], P(('clip', 'trow'), 'tcol'), parts along dimension 0
The draws below stay inside these ranges and needn't reach their ends.
There are 2 independent parts, one for each index of `clip`. The reference program is written for one: setup_inputs(seed, part) draws one part's arguments, and reference() takes and returns one part's arrays. A program takes and returns all parts, laid end to end along the dimension named above; an argument that names none is the same for every part. Nothing has to cross between parts.
All inputs are finite; a program needn't handle non-finite values.
Results may differ from the reference program's by a relative error of at most 0.0084.
Values sent between devices are 32-bit elements; how exact they have to be, the bound alone decides.
No kernel may reach another device: no remote copies, remote signals or barrier semaphores. Data moves between devices by JAX's collectives and lax.ppermute only.
A program may use at most 128 MiB of HBM per device.

```python
import math
import jax
import jax.numpy as jnp
from jax import lax

C = 8
NY = 8192
KY = 48
LAYERS = 2
ROW_DEV = 128
MODES2 = 4608
NX = 1024
N_TROW = 8


def block_scale(key, shape, cuts, smallest, high):
    gain = 1.0
    for dim, shards_of in cuts:
        steps = jax.random.uniform(jax.random.fold_in(jax.random.fold_in(key, 6), dim), (shards_of,), jnp.float32, smallest / len(cuts), high / len(cuts))
        gain = gain * jnp.repeat(jnp.exp(steps), shape[dim] // shards_of).reshape((-1,) + (1,) * (len(shape) - 1 - dim))
    return gain


def bell_draw(key, shape, deviation, limit, shards=(), held_as=jnp.bfloat16):
    values = deviation * jax.random.normal(key, shape, jnp.float32)
    if shards:
        values = values * block_scale(key, shape, shards, -0.22, 0.18)
    return jnp.clip(values, -limit, limit).astype(held_as)


def setup_inputs(seed: int = 0, part: int = 0) -> dict:
    keys = jax.random.split(jax.random.key(seed), 5)
    part_splits = jax.random.split(jax.random.fold_in(keys[4], part), 5)
    return {
        "field": bell_draw(part_splits[0], (C, NX, NY), 1.0, 6.0, ((1, 8), (2, 2))),
        "pointwise": bell_draw(keys[1], (LAYERS, C, C), C ** -0.5, 2.0),
        "mixing": bell_draw(keys[2], (LAYERS, 2, C, C, MODES2), C ** -0.5, 2.0),
        "project": bell_draw(keys[3], (C,), C ** -0.5, 2.0),
    }


def column_table(start, count, total, modes):
    columns = start + jnp.arange(count, dtype=jnp.int32)
    freqs = jnp.arange(modes, dtype=jnp.int32)
    phase = columns[:, None] * freqs[None, :] % total
    angle = phase.astype(jnp.float32) * (2.0 * math.pi / total)
    return jnp.concatenate([jnp.cos(angle), -jnp.sin(angle)], axis=1).astype(jnp.bfloat16)

def row_tables(start, count, total, modes):
    rows_here = start + jnp.arange(count, dtype=jnp.int32)
    freqs = jnp.arange(2 * modes, dtype=jnp.int32)
    freqs = jnp.where(freqs < modes, freqs, freqs + (total - 2 * modes)).astype(jnp.int32)
    phase = freqs[:, None] * rows_here[None, :] % total
    angle = phase.astype(jnp.float32) * (2.0 * math.pi / total)
    return (jnp.cos(angle), jnp.sin(angle))

def forward_spectrum(values, row_start, total_rows, col_start, total_cols, modes):
    channels, rows_here, cols_here = values.shape
    table = column_table(col_start, cols_here, total_cols, modes)
    partial_value = jnp.dot(values.reshape(channels * rows_here, cols_here), table, preferred_element_type=jnp.float32)
    partial_value = partial_value.reshape(channels, rows_here, 2 * modes).transpose(1, 0, 2).reshape(rows_here, channels * 2 * modes)
    cosine, sine = row_tables(row_start, rows_here, total_rows, modes)
    stacked = jnp.dot(jnp.concatenate([cosine, sine], axis=0), partial_value, precision=lax.Precision.HIGHEST, preferred_element_type=jnp.float32)
    stacked = stacked.reshape(2, 2 * modes, channels, 2, modes)
    real_part = stacked[0, :, :, 0] + stacked[1, :, :, 1]
    imag_part = stacked[0, :, :, 1] - stacked[1, :, :, 0]
    spectrum = jnp.stack([real_part, imag_part]).transpose(0, 2, 1, 3).reshape(2, channels, 2 * modes * modes)
    return spectrum * (1.0 / math.sqrt(total_rows * total_cols))

def mix_modes(spectrum, weights_in):
    weights = weights_in.astype(jnp.float32)
    real_part = lax.optimization_barrier(jnp.sum(weights[0] * spectrum[0][None], axis=1)) - lax.optimization_barrier(jnp.sum(weights[1] * spectrum[1][None], axis=1))
    imag_part = lax.optimization_barrier(jnp.sum(weights[0] * spectrum[1][None], axis=1)) + lax.optimization_barrier(jnp.sum(weights[1] * spectrum[0][None], axis=1))
    return jnp.stack([real_part, imag_part])

def inverse_field(mixed, row_start, rows_here, total_rows, col_start, cols_here, total_cols, modes):
    channels = mixed.shape[1]
    arranged = mixed.reshape(2, channels, 2 * modes, modes).transpose(2, 0, 1, 3).reshape(2 * modes, 2 * channels * modes)
    cosine, sine = row_tables(row_start, rows_here, total_rows, modes)
    table = jnp.concatenate([cosine.T, sine.T], axis=0)
    stacked = jnp.dot(table, arranged, precision=lax.Precision.HIGHEST, preferred_element_type=jnp.float32)
    stacked = stacked.reshape(2, rows_here, 2, channels, modes)
    real_part = stacked[0, :, 0] - stacked[1, :, 1]
    imag_part = stacked[1, :, 0] + stacked[0, :, 1]
    hidden = jnp.stack([real_part, imag_part], axis=2).transpose(1, 0, 2, 3).reshape(channels * rows_here, 2 * modes).astype(jnp.bfloat16)
    col_tab = column_table(col_start, cols_here, total_cols, modes)
    values = jnp.dot(hidden, col_tab.T, preferred_element_type=jnp.float32) * (1.0 / modes)
    return values.reshape(channels, rows_here, cols_here)

def layer_update(values, weights, mixed, row_start, total_rows, col_start, total_cols, modes):
    channels, rows_here, cols_here = values.shape
    spectral = inverse_field(mixed, row_start, rows_here, total_rows, col_start, cols_here, total_cols, modes)
    local = jnp.dot(weights, values.reshape(channels, rows_here * cols_here), preferred_element_type=jnp.float32)
    return jnp.tanh(local.reshape(channels, rows_here, cols_here) + spectral)

def reference(field, pointwise, mixing, project):
    total_rows = ROW_DEV * N_TROW
    current = field
    result = None
    for layer in range(LAYERS):

        def add_block(carry, index):
            start = (index * ROW_DEV).astype(jnp.int32)
            piece = lax.dynamic_slice_in_dim(current, start, ROW_DEV, 1)
            return (carry + forward_spectrum(piece, start, total_rows, 0, NY, KY), None)
        empty = jnp.zeros((2, C, MODES2), jnp.float32)
        spectrum, ignored = lax.scan(add_block, empty, jnp.arange(N_TROW, dtype=jnp.int32))
        mixed = mix_modes(spectrum, mixing[layer])
        last = layer + 1 == LAYERS

        def one_block(index):
            start = (index * ROW_DEV).astype(jnp.int32)
            piece = lax.dynamic_slice_in_dim(current, start, ROW_DEV, 1)
            updated = layer_update(piece, pointwise[layer], mixed, start, total_rows, 0, NY, KY)
            if last:
                return lax.optimization_barrier(jnp.sum(project.astype(jnp.float32)[:, None, None] * updated, axis=0)).astype(jnp.bfloat16)
            return updated.astype(jnp.bfloat16)
        pieces = lax.map(one_block, jnp.arange(N_TROW, dtype=jnp.int32))
        if last:
            result = pieces.reshape(total_rows, NY)
        else:
            current = pieces.transpose(1, 0, 2, 3).reshape(C, total_rows, NY)
    return result
```

```python
import functools
import math

import jax
import jax.numpy as jnp
import ml_dtypes
import numpy as np
from jax import lax
from jax.experimental import pallas as pl
from jax.experimental.pallas import tpu as pltpu
from jax.sharding import PartitionSpec as P

KY = 48
LAYERS = 2
LANES = 128
HALF = 64
HOLE = HALF - KY
GROUP = 16
TILE = 512
HIGHEST = lax.Precision.HIGHEST
VMEM_LIMIT = 48 * 1024 * 1024


@functools.cache
def column_tables(total):
    phase = np.arange(total)[:, None] * np.arange(KY)[None, :] % total
    angle = phase.astype(np.float64) * (2.0 * math.pi / total)
    table = np.zeros((total, LANES), np.float32)
    table[:, :KY] = np.cos(angle)
    table[:, HALF : HALF + KY] = -np.sin(angle)
    return table.astype(ml_dtypes.bfloat16)


@functools.cache
def row_tables(total):
    freqs = np.arange(2 * KY)
    freqs = np.where(freqs < KY, freqs, freqs + (total - 2 * KY))
    angle = (freqs[:, None] * np.arange(total)[None, :] % total).astype(np.float64) * (2.0 * math.pi / total)
    return np.cos(angle), np.sin(angle)


def forward_rows(total_rows, rows, total_cols):
    cosine, sine = row_tables(total_rows)
    scale = 1.0 / math.sqrt(total_rows * total_cols)
    both = np.stack([cosine, sine]).reshape(2, 2 * KY, total_rows // rows, rows) * scale
    return both.transpose(2, 1, 0, 3).reshape(-1, 2 * KY, 2 * rows).astype(np.float32)


def inverse_rows(total_rows, rows):
    cosine, sine = row_tables(total_rows)
    both = np.stack([cosine, sine]).reshape(2, 2 * KY, total_rows // rows, rows)
    return both.transpose(2, 3, 0, 1).reshape(-1, rows, 4 * KY).astype(np.float32)


def lane_index(shape):
    return lax.broadcasted_iota(jnp.int32, shape, len(shape) - 1)


def pack(spectrum):
    keep = 3 * KY // 2
    part = keep // 3
    tail = spectrum[keep:]
    hole = (lane_index((part, LANES)) % HALF) >= KY
    rows = []
    for j in range(3):
        moved = pltpu.roll(tail, KY - HOLE * j, 1)
        rows.append(jnp.where(hole, moved, spectrum[part * j : part * (j + 1)]))
    return jnp.concatenate(rows, axis=0)


def unpack(packed):
    part = KY // 2
    lane = lane_index((part, LANES)) % HALF
    tail = jnp.zeros((part, LANES), jnp.float32)
    for j in range(3):
        moved = pltpu.roll(packed[part * j : part * (j + 1)], LANES - (KY - HOLE * j), 1)
        tail = jnp.where(lane // HOLE == j, moved, tail)
    return jnp.concatenate([packed, tail], axis=0)


def row_transform(table, partial):
    sign = jnp.where(lane_index(partial.shape) < HALF, 1.0, -1.0)
    turned = pltpu.roll(partial, HALF, 1) * sign
    return jnp.dot(
        table,
        jnp.concatenate([partial, turned], axis=0),
        precision=HIGHEST,
        preferred_element_type=jnp.float32,
    )


def first_kernel(where_ref, v_ref, e_ref, rows_ref, out_ref):
    channels, rows, cols = v_ref.shape
    partial = jnp.dot(
        v_ref[...].reshape(channels * rows, cols), e_ref[...], preferred_element_type=jnp.float32
    )
    for c in range(channels):
        out_ref[c] = pack(row_transform(rows_ref[0], partial[c * rows : (c + 1) * rows]))


def hidden_field(s_ref, w_ref, inv_ref, h_ref):
    channels = s_ref.shape[0]
    spectrum = [unpack(s_ref[c]) for c in range(channels)]
    swapped = [pltpu.roll(s, HALF, 1) for s in spectrum]
    low = lane_index((2 * KY, LANES)) < HALF
    sign = jnp.where(low, -1.0, 1.0)
    for o in range(channels):
        direct = crossed = None
        for c in range(channels):
            weight = w_ref[o, c].astype(jnp.float32)
            a, b = weight * spectrum[c], weight * swapped[c]
            direct = a if direct is None else direct + a
            crossed = b if crossed is None else crossed + b
        mixed = jnp.where(low, direct - pltpu.roll(direct, HALF, 1), crossed + pltpu.roll(crossed, HALF, 1))
        turned = pltpu.roll(mixed, HALF, 1) * sign
        hidden = jnp.dot(
            inv_ref[0],
            jnp.concatenate([mixed, turned], axis=0),
            precision=HIGHEST,
            preferred_element_type=jnp.float32,
        )
        h_ref[o] = hidden.astype(jnp.bfloat16)


def layer_kernel(last, where_ref, s_ref, w_ref, inv_ref, v_ref, et_ref, point_ref, *rest):
    if last:
        project_ref, out_ref, h_ref = rest
    else:
        e_ref, rows_ref, out_ref, next_ref, h_ref, g_ref = rest
    channels, group, cols = v_ref.shape
    step = pl.program_id(0)

    @pl.when(step == 0)
    def _():
        hidden_field(s_ref, w_ref, inv_ref, h_ref)

    here = pl.ds(pl.multiple_of(step * group, group), group)
    left = jnp.concatenate(
        [h_ref[:, here, :].reshape(channels * group, LANES), point_ref[...]], axis=1
    )
    tile = min(TILE, cols)

    total = None
    for n in range(cols // tile):
        span = pl.ds(n * tile, tile)
        right = jnp.concatenate(
            [et_ref[:, span], v_ref[:, :, span].reshape(channels * group, tile)], axis=0
        )
        z = jnp.tanh(jnp.dot(left, right, preferred_element_type=jnp.float32) * (1.0 / KY))
        if last:
            z = z.reshape(channels, group, tile)
            image = project_ref[0] * z[0]
            for c in range(1, channels):
                image = image + project_ref[c] * z[c]
            out_ref[:, span] = image.astype(out_ref.dtype)
        else:
            z = z.astype(jnp.bfloat16)
            out_ref[:, :, span] = z.reshape(channels, group, tile)
            part = jnp.dot(z, e_ref[span, :], preferred_element_type=jnp.float32)
            total = part if total is None else total + part
    if not last:
        g_ref[:, here, :] = total.reshape(channels, group, LANES)

        @pl.when(step == pl.num_programs(0) - 1)
        def _():
            for c in range(channels):
                next_ref[c] = pack(row_transform(rows_ref[0], g_ref[c]))


def params():
    return pltpu.CompilerParams(dimension_semantics=("arbitrary",), vmem_limit_bytes=VMEM_LIMIT)


def packed_shape(channels):
    return (channels, 3 * KY // 2, LANES)


def first_layer_spectrum(where, field, e, rows_table):
    channels, rows, cols = field.shape
    block = 1
    return pl.pallas_call(
        first_kernel,
        out_shape=jax.ShapeDtypeStruct(packed_shape(channels), jnp.float32),
        grid_spec=pltpu.PrefetchScalarGridSpec(
            num_scalar_prefetch=1,
            grid=(channels // block,),
            in_specs=[
                pl.BlockSpec((block, rows, cols), lambda i, w: (i, 0, 0)),
                pl.BlockSpec((cols, LANES), lambda i, w: (w[1], 0)),
                pl.BlockSpec((1, 2 * KY, 2 * rows), lambda i, w: (w[0], 0, 0)),
            ],
            out_specs=pl.BlockSpec((block,) + packed_shape(channels)[1:], lambda i, w: (i, 0, 0)),
        ),
        compiler_params=params(),
    )(where, field, e, rows_table)


def layer(where, spectrum, weights, inv_table, values, et, point, tail, last):
    channels, rows, cols = values.shape
    in_specs = [
        pl.BlockSpec(spectrum.shape, lambda i, w: (0, 0, 0)),
        pl.BlockSpec(weights.shape, lambda i, w: (0, 0, 0, 0)),
        pl.BlockSpec((1, rows, 4 * KY), lambda i, w: (w[0], 0, 0)),
        pl.BlockSpec((channels, GROUP, cols), lambda i, w: (0, i, 0)),
        pl.BlockSpec((LANES, cols), lambda i, w: (0, w[1])),
        pl.BlockSpec(point.shape, lambda i, w: (0, 0)),
    ]
    scratch = [pltpu.VMEM((channels, rows, LANES), jnp.bfloat16)]
    if last:
        in_specs.append(pl.BlockSpec(memory_space=pltpu.SMEM))
        out_shape = jax.ShapeDtypeStruct((rows, cols), jnp.bfloat16)
        out_specs = pl.BlockSpec((GROUP, cols), lambda i, w: (i, 0))
    else:
        in_specs += [
            pl.BlockSpec((cols, LANES), lambda i, w: (w[1], 0)),
            pl.BlockSpec((1, 2 * KY, 2 * rows), lambda i, w: (w[0], 0, 0)),
        ]
        out_shape = (
            jax.ShapeDtypeStruct(values.shape, jnp.bfloat16),
            jax.ShapeDtypeStruct(spectrum.shape, jnp.float32),
        )
        out_specs = (
            pl.BlockSpec((channels, GROUP, cols), lambda i, w: (0, i, 0)),
            pl.BlockSpec(spectrum.shape, lambda i, w: (0, 0, 0)),
        )
        scratch.append(pltpu.VMEM((channels, rows, LANES), jnp.float32))
    return pl.pallas_call(
        functools.partial(layer_kernel, last),
        out_shape=out_shape,
        grid_spec=pltpu.PrefetchScalarGridSpec(
            num_scalar_prefetch=1,
            grid=(rows // GROUP,),
            in_specs=in_specs,
            out_specs=out_specs,
            scratch_shapes=scratch,
        ),
        compiler_params=params(),
    )(where, spectrum, weights, inv_table, values, et, point, *tail)


def swap_pairs(x, axis, bit):
    size = lax.axis_size(axis)
    return lax.ppermute(x, axis, [(i, i ^ bit) for i in range(size)])


def halve(x, axis, bit):
    side = lax.axis_index(axis) // bit % 2
    half = x.shape[0] // 2
    kept = lax.dynamic_slice_in_dim(x, side * half, half, 0)
    sent = lax.dynamic_slice_in_dim(x, (1 - side) * half, half, 0)
    return kept + swap_pairs(sent, axis, bit)


def double(x, axis, bit):
    side = lax.axis_index(axis) // bit % 2
    other = swap_pairs(x, axis, bit)
    return jnp.where(side == 0, jnp.concatenate([x, other]), jnp.concatenate([other, x]))


def sum_all(x):
    trow, tcol = lax.axis_size("trow"), lax.axis_size("tcol")
    if tcol != 2 or trow < 2 or trow & (trow - 1):
        return lax.psum(x, ("trow", "tcol"))
    x = halve(x, "tcol", 1)
    x = halve(x, "trow", 1)
    bit = 2
    while bit < trow:
        x = x + swap_pairs(x, "trow", bit)
        bit *= 2
    x = double(x, "trow", 1)
    return double(x, "tcol", 1)


def mixing_table(weights):
    channels = weights.shape[1]
    split = weights.reshape(2, channels, channels, 2 * KY, KY)
    padded = jnp.pad(split, ((0, 0), (0, 0), (0, 0), (0, 0), (0, HOLE)))
    return jnp.concatenate([padded[0], padded[1]], axis=-1)


def body(field, pointwise, mixing, project):
    rows, cols = field.shape[1:]
    total_rows = rows * lax.axis_size("trow")
    total_cols = cols * lax.axis_size("tcol")
    where = jnp.stack([lax.axis_index("trow"), lax.axis_index("tcol")]).astype(jnp.int32)
    table = column_tables(total_cols)
    e, et = jnp.asarray(table), jnp.asarray(np.ascontiguousarray(table.T))
    ahead = jnp.asarray(forward_rows(total_rows, rows, total_cols))
    back = jnp.asarray(inverse_rows(total_rows, rows))
    eye = jnp.eye(GROUP, dtype=jnp.bfloat16)
    points = [jnp.kron(pointwise[i] * KY, eye) for i in range(LAYERS)]
    mixes = [mixing_table(mixing[i]) for i in range(LAYERS)]

    current = field
    spectrum = first_layer_spectrum(where, field, e, ahead)
    for i in range(LAYERS):
        summed = sum_all(spectrum)
        if i + 1 == LAYERS:
            tail = (project.astype(jnp.float32),)
            return layer(where, summed, mixes[i], back, current, et, points[i], tail, True)
        current, spectrum = layer(where, summed, mixes[i], back, current, et, points[i], (e, ahead), False)


def solution(mesh):
    in_specs = (P(None, ("clip", "trow"), "tcol"), P(), P(), P())
    out_specs = P(("clip", "trow"), "tcol")
    return jax.shard_map(body, mesh=mesh, in_specs=in_specs, out_specs=out_specs, check_vma=False)
```
